128 devices in a mesh: ctx: 16 (over x, z), pp: 4 (over y_lo, core), tp: 2 (over y_hi).
Axes of the slice: x: 4, y: 4 (y_hi: 2, y_lo: 2; y = y_hi * 2 + y_lo), z: 4, core: 2. Of those that a mesh axis runs over, the one named last changes fastest.
Arguments:
- next_grad: bfloat16 [4, 2048, 6144], P('pp', ('ctx', 'tp')), may hold values from -6 to 6
- queries: bfloat16 [4, 2048, 6144], P('pp', 'ctx', 'tp'), may hold values from -6 to 6
- keys: bfloat16 [4, 2048, 6144], P('pp', 'ctx', 'tp'), may hold values from -6 to 6
- values: bfloat16 [4, 2048, 6144], P('pp', 'ctx', 'tp'), may hold values from -6 to 6
- outputs: bfloat16 [4, 2048, 6144], P('pp', 'ctx', 'tp'), may hold values from -6 to 6
- log_sums: float32 [4, 2048, 48], P('pp', 'ctx', 'tp'), may hold values from 4 to 7
- part_length: int32 [4], P('pp'), may hold values from 64 to 1984, as said below
Outputs:
- query_grad: bfloat16 [4, 2048, 6144], P('pp', 'ctx', 'tp')
- key_grad: bfloat16 [4, 2048, 6144], P('pp', 'ctx', 'tp')
- value_grad: bfloat16 [4, 2048, 6144], P('pp', 'ctx', 'tp')
The draws below stay inside these ranges and needn't reach their ends.
Inputs may be any that keep to these rules, and one draw needn't show every extreme that they name: `part_length`: each section's sequence has its own part-A length; the shortest and the longest allowed both occur in every draw.
All inputs are finite; a program needn't handle non-finite values.
Results may differ from the reference program's by a relative error of at most 0.0051.
Values may be sent and summed in bfloat16 or wider, within the bound.
No kernel may reach another device: no remote copies, remote signals or barrier semaphores. Data moves between devices by JAX's collectives and lax.ppermute only.
A program may use at most 192 MiB of HBM per device.

```python
import jax
import jax.numpy as jnp
from jax import lax

HEADS = 48
HDIM = 128
SEQ_DEV = 128
SECTIONS = 4
TOKENS = 2048


def draw_part_length(key, part):
    key = jax.random.fold_in(key, 7)
    first_key, second_key = jax.random.split(key)
    lowest = SEQ_DEV // 2
    highest = TOKENS - SEQ_DEV // 2
    lengths = jax.random.randint(first_key, (SECTIONS,), lowest, highest + 1, dtype=jnp.int32)
    shuffled = jax.random.permutation(second_key, SECTIONS)
    lengths = lengths.at[shuffled[0]].set(lowest)
    return lengths.at[shuffled[1]].set(highest)


def level_of(own_key, extent, cuts, least, high):
    gain = 1.0
    for axis_at, parts in cuts:
        steps = jax.random.uniform(jax.random.fold_in(jax.random.fold_in(own_key, 6), axis_at), (parts,), jnp.float32, least / len(cuts), high / len(cuts))
        gain = gain * jnp.repeat(jnp.exp(steps), extent[axis_at] // parts).reshape((-1,) + (1,) * (len(extent) - 1 - axis_at))
    return gain


def scatter_about(key, shape, deviation, most, cuts=(), kind=jnp.bfloat16):
    result = jax.random.normal(key, shape, jnp.float32) * deviation
    if len(cuts) > 0:
        result = level_of(key, shape, cuts, -0.22, 0.18) * result
    return jnp.clip(result, min=-most, max=most).astype(kind)


def setup_inputs(seed: int = 0) -> dict:
    streams_of = jax.random.split(jax.random.key(seed), 8)
    next_grad = scatter_about(streams_of[0], (SECTIONS, TOKENS, HEADS * HDIM), 1.0, 6.0, ((0, 4), (1, 32)))
    queries = scatter_about(streams_of[1], (SECTIONS, TOKENS, HEADS * HDIM), 1.0, 6.0, ((0, 4), (1, 16), (2, 2)))
    keys = scatter_about(streams_of[2], (SECTIONS, TOKENS, HEADS * HDIM), 1.0, 6.0, ((0, 4), (1, 16), (2, 2)))
    values = scatter_about(streams_of[3], (SECTIONS, TOKENS, HEADS * HDIM), 1.0, 6.0, ((0, 4), (1, 16), (2, 2)))
    outputs = scatter_about(streams_of[4], (SECTIONS, TOKENS, HEADS * HDIM), 1.0, 6.0, ((0, 4), (1, 16), (2, 2)))
    log_sums = jnp.clip(4.0 + 3.0 * jax.random.uniform(streams_of[5], (SECTIONS, TOKENS, HEADS), jnp.float32) ** level_of(streams_of[5], (SECTIONS, TOKENS, HEADS), ((0, 4), (1, 16), (2, 2)), -0.2, 0.2), 4.0, 7.0)
    part_length = draw_part_length(jax.random.fold_in(streams_of[7], 71), 0)
    return dict(next_grad=next_grad, queries=queries, keys=keys, values=values, outputs=outputs, log_sums=log_sums, part_length=part_length)


def head_terms(pieces, part_len, factor):
    query_rows, key_rows, value_rows, grad_rows, out_rows, sum_rows = pieces
    positions = jnp.arange(query_rows.shape[0], dtype=jnp.int32)
    visible = jnp.logical_or(positions[None, :] < part_len, positions[None, :] <= positions[:, None])
    scores = jnp.dot(query_rows, key_rows.T, preferred_element_type=jnp.float32) * factor
    weights = jnp.where(visible, jnp.exp(scores - sum_rows[:, None]), jnp.float32(0.0))
    deltas = jnp.sum(grad_rows.astype(jnp.float32) * out_rows.astype(jnp.float32), axis=1)
    weight_grads = jnp.dot(grad_rows, value_rows.T, preferred_element_type=jnp.float32)
    score_grads = (weights * (weight_grads - deltas[:, None]) * factor).astype(jnp.bfloat16)
    query_grad = jnp.dot(score_grads, key_rows, preferred_element_type=jnp.float32).astype(jnp.bfloat16)
    key_grad = jnp.dot(score_grads.T, query_rows, preferred_element_type=jnp.float32).astype(jnp.bfloat16)
    weights_low = weights.astype(jnp.bfloat16)
    value_grad = jnp.dot(weights_low.T, grad_rows, preferred_element_type=jnp.float32).astype(jnp.bfloat16)
    return query_grad, key_grad, value_grad


def split_heads(matrix):
    return jnp.transpose(matrix.reshape(TOKENS, HEADS, HDIM), (1, 0, 2))


def join_heads(stacked):
    return jnp.transpose(stacked, (1, 0, 2)).reshape(TOKENS, HEADS * HDIM)


def reference(next_grad, queries, keys, values, outputs, log_sums, part_length):
    grad_out = jnp.roll(next_grad, -1, axis=0)
    factor = HDIM ** -0.5
    query_list = []
    key_list = []
    value_list = []
    for section in range(SECTIONS):
        part_len = part_length[section]

        def per_head(pieces):
            return head_terms(pieces, part_len, factor)

        stacked = (split_heads(queries[section]), split_heads(keys[section]), split_heads(values[section]),
                   split_heads(grad_out[section]), split_heads(outputs[section]), jnp.transpose(log_sums[section]))
        head_query, head_key, head_value = lax.map(per_head, stacked)
        query_list.append(join_heads(head_query))
        key_list.append(join_heads(head_key))
        value_list.append(join_heads(head_value))
    return jnp.stack(query_list), jnp.stack(key_list), jnp.stack(value_list)
```

```python
import functools

import jax
import jax.numpy as jnp
from jax import lax
from jax.experimental import pallas as pl
from jax.experimental.pallas import tpu as pltpu
from jax.sharding import PartitionSpec as P

HDIM = 128
LOG2E = 1.4426950408889634
FACTOR = HDIM ** (-0.5)
QTILE = 512
KTILE = 1024


def dot_nt(a, b):
    return lax.dot_general(a, b, (((1,), (1,)), ((), ())), preferred_element_type=jnp.float32)


def dot_nn(a, b):
    return lax.dot_general(a, b, (((1,), (0,)), ((), ())), preferred_element_type=jnp.float32)


def dot_tn(a, b):
    return lax.dot_general(a, b, (((0,), (0,)), ((), ())), preferred_element_type=jnp.float32)


def attention_kernel(meta_ref, qkv, grads, stat, out, dq_acc, dk_acc, dv_acc, *, blocks, seq):
    part_len = meta_ref[0]
    half = meta_ref[1]
    span = QTILE // seq
    query_tiles = blocks // span

    def one_head(rows, q_at, k_at, v_at, g_at, which, dq_at, dk_at, dv_at):
        key_span = KTILE // rows
        dq_acc[...] = jnp.zeros_like(dq_acc)

        def key_tile(kt, carry):
            first = kt * key_span
            key_rows = qkv[pl.ds(first, key_span), k_at : k_at + rows, :].reshape(KTILE, HDIM)
            value_rows = qkv[pl.ds(first, key_span), v_at : v_at + rows, :].reshape(KTILE, HDIM)
            index = lax.broadcasted_iota(jnp.int32, (KTILE, 1), 0)
            if rows == seq:
                key_pos = first * seq + index
            else:
                key_pos = (first + index // rows) * seq + half * rows + index % rows
            key_pos = jnp.where(key_pos < part_len, -1, key_pos)
            dk_acc[...] = jnp.zeros_like(dk_acc)
            dv_acc[...] = jnp.zeros_like(dv_acc)

            def query_tile(qt, carry):
                at = qt * span
                query_rows = qkv[pl.ds(at, span), q_at : q_at + seq, :].reshape(QTILE, HDIM)
                grad_rows = grads[pl.ds(at, span), g_at : g_at + seq, :].reshape(QTILE, HDIM)
                log_sum = stat[2 * which, pl.ds(qt, 1), :]
                delta = stat[2 * which + 1, pl.ds(qt, 1), :]
                scores = dot_nt(key_rows, query_rows) * (FACTOR * LOG2E) - log_sum
                query_pos = at * seq + lax.broadcasted_iota(jnp.int32, (1, QTILE), 1)
                weights = jnp.where(key_pos <= query_pos, jnp.exp2(scores), 0.0)
                weight_grads = dot_nt(value_rows, grad_rows)
                score_grads = (weights * (weight_grads - delta) * FACTOR).astype(jnp.bfloat16)
                dv_acc[...] += dot_nn(weights.astype(jnp.bfloat16), grad_rows)
                dk_acc[...] += dot_nn(score_grads, query_rows)
                where = pl.ds(pl.multiple_of(at * seq, QTILE), QTILE)
                dq_acc[where, :] += dot_tn(score_grads, key_rows)
                return carry

            lax.fori_loop(0, query_tiles, query_tile, 0)
            shape = (key_span, rows, HDIM)
            out[pl.ds(first, key_span), dk_at : dk_at + rows, :] = dk_acc[...].astype(jnp.bfloat16).reshape(shape)
            out[pl.ds(first, key_span), dv_at : dv_at + rows, :] = dv_acc[...].astype(jnp.bfloat16).reshape(shape)
            return carry

        lax.fori_loop(0, blocks // key_span, key_tile, 0)
        out[:, dq_at : dq_at + seq, :] = dq_acc[...].astype(jnp.bfloat16).reshape(blocks, seq, HDIM)

    half_rows = seq // 2
    one_head(seq, 0, seq, 2 * seq, 0, 0, 0, seq, 2 * seq)
    one_head(half_rows, 3 * seq, 4 * seq, 4 * seq + half_rows, seq, 1, 3 * seq, 4 * seq, 4 * seq + half_rows)


def attention(meta, qkv, grads, stat):
    blocks = qkv.shape[0]
    seq = qkv.shape[1] // 5
    total = blocks * seq
    tiles = stat.reshape(4, total // QTILE, QTILE)
    return pl.pallas_call(
        functools.partial(attention_kernel, blocks=blocks, seq=seq),
        out_shape=jax.ShapeDtypeStruct((blocks, 5 * seq, HDIM), jnp.bfloat16),
        in_specs=[pl.BlockSpec(memory_space=pltpu.SMEM)] + [pl.BlockSpec(memory_space=pltpu.VMEM)] * 3,
        out_specs=pl.BlockSpec(memory_space=pltpu.VMEM),
        scratch_shapes=[
            pltpu.VMEM((total, HDIM), jnp.float32),
            pltpu.VMEM((KTILE, HDIM), jnp.float32),
            pltpu.VMEM((KTILE, HDIM), jnp.float32),
        ],
        compiler_params=pltpu.CompilerParams(vmem_limit_bytes=48 << 20),
        cost_estimate=pl.CostEstimate(
            flops=15 * total * total * HDIM, bytes_accessed=8 << 20, transcendentals=3 * total * total // 2
        ),
    )(meta, qkv, grads, tiles)


def by_head(rows):
    return jnp.transpose(rows.reshape(rows.shape[0], -1, HDIM), (1, 0, 2))


def three_parts(x):
    high = lax.reduce_precision(x, 8, 7)
    rest = x - high
    middle = lax.reduce_precision(rest, 8, 7)
    return [high, middle, rest - middle]


def per_device(next_grad, queries, keys, values, outputs, log_sums, part_length):
    devices = lax.axis_size("ctx")
    sections = lax.axis_size("pp")
    ctx = lax.axis_index("ctx")
    tp = lax.axis_index("tp")
    seq, width = queries.shape[1:]
    local_rows = next_grad.shape[1]
    own_cols = lax.dynamic_slice_in_dim(next_grad[0], tp * width, width, 1)
    other_cols = lax.dynamic_slice_in_dim(next_grad[0], (1 - tp) * width, width, 1)
    route = [((p + 1) % sections, p) for p in range(sections)]
    cross = [(2 * a + t, 2 * b + 1 - t) for a, b in route for t in range(2)]
    near = lax.ppermute(own_cols, "pp", route)
    far = lax.ppermute(other_cols, ("pp", "tp"), cross)

    def spread(rows, shared_half):
        heads = by_head(rows)
        shared = heads[devices:]
        if shared_half:
            return heads[:devices], shared.reshape(devices, seq // 2, HDIM)
        return heads[:devices], jnp.repeat(shared, 2, axis=0)

    q_whole, q_shared = spread(queries[0], False)
    k_whole, k_shared = spread(keys[0], True)
    v_whole, v_shared = spread(values[0], True)
    packed = jnp.concatenate([q_whole, k_whole, v_whole, q_shared, k_shared, v_shared], axis=1)
    qkv = lax.all_to_all(packed, "ctx", 0, 0, tiled=True)

    first = jnp.where(tp == 0, near, far)
    second = jnp.where(tp == 0, far, near)
    grad_rows = jnp.concatenate([first, second], axis=0)
    heads = width // HDIM
    deltas = jnp.sum(
        (grad_rows.astype(jnp.float32) * outputs[0].astype(jnp.float32)).reshape(seq, heads, HDIM), axis=2
    )
    g_whole, g_shared = spread(grad_rows, False)

    def stat_rows(x):
        x = jnp.transpose(x)
        both = [x[:devices], jnp.repeat(x[devices:], 2, axis=0)]
        return [jnp.stack(three_parts(y), axis=1) for y in both]

    l_whole, l_shared = stat_rows(log_sums[0] * LOG2E)
    d_whole, d_shared = stat_rows(deltas)
    stats = jnp.concatenate([l_whole, d_whole, l_shared, d_shared], axis=1)
    stats = jnp.pad(stats, ((0, 0), (0, 4), (0, 0))).astype(jnp.bfloat16)
    packed = jnp.concatenate([g_whole, g_shared, stats], axis=1)
    grads = lax.all_to_all(packed, "ctx", 0, 0, tiled=True)
    parts = grads[:, 2 * seq : 2 * seq + 12, :].astype(jnp.float32).reshape(devices, 4, 3, seq)
    stat = jnp.transpose(parts[:, :, 0] + parts[:, :, 1] + parts[:, :, 2], (1, 0, 2)).reshape(4, devices * seq)

    meta = jnp.stack([part_length[0], ctx % 2])
    mixed = attention(meta, qkv, grads, stat)
    back = lax.all_to_all(mixed, "ctx", 0, 0, tiled=True)

    def gather(whole, shared):
        joined = jnp.concatenate([whole, shared], axis=0)
        return jnp.transpose(joined, (1, 0, 2)).reshape(1, seq, width)

    halves = back[:, 3 * seq : 4 * seq].astype(jnp.float32).reshape(devices // 2, 2, seq, HDIM)
    dq_shared = (halves[:, 0] + halves[:, 1]).astype(jnp.bfloat16)
    dk_shared = back[:, 4 * seq : 4 * seq + seq // 2].reshape(devices // 2, seq, HDIM)
    dv_shared = back[:, 4 * seq + seq // 2 :].reshape(devices // 2, seq, HDIM)
    return (
        gather(back[:, :seq], dq_shared),
        gather(back[:, seq : 2 * seq], dk_shared),
        gather(back[:, 2 * seq : 3 * seq], dv_shared),
    )


def solution(mesh):
    rows = P("pp", "ctx", "tp")
    return jax.shard_map(
        per_device,
        mesh=mesh,
        in_specs=(P("pp", ("ctx", "tp"), None), rows, rows, rows, rows, rows, P("pp")),
        out_specs=(rows, rows, rows),
        check_vma=False,
    )
```

```python
import functools

import jax
import jax.numpy as jnp
from jax import lax
from jax.experimental import pallas as pl
from jax.experimental.pallas import tpu as pltpu
from jax.sharding import PartitionSpec as P

HDIM = 128
LOG2E = 1.4426950408889634
FACTOR = HDIM ** (-0.5)
QTILE = 1024
KTILE = 1024
STAT = 16
VMEM = pl.BlockSpec(memory_space=pltpu.VMEM)
SMEM = pl.BlockSpec(memory_space=pltpu.SMEM)
PARAMS = pltpu.CompilerParams(vmem_limit_bytes=48 << 20)


def dot_nt(a, b):
    return lax.dot_general(a, b, (((1,), (1,)), ((), ())), preferred_element_type=jnp.float32)


def dot_nn(a, b):
    return lax.dot_general(a, b, (((1,), (0,)), ((), ())), preferred_element_type=jnp.float32)


def three_parts(x):
    high = x.astype(jnp.bfloat16).astype(jnp.float32)
    rest = x - high
    middle = rest.astype(jnp.bfloat16).astype(jnp.float32)
    return high, middle, rest - middle


def stat_rows(whole, shared):
    rows = [*whole, *shared, jnp.zeros((STAT - 6, HDIM), jnp.float32)]
    return jnp.concatenate(rows, axis=0).astype(jnp.bfloat16)


def pack_kernel(queries, keys, values, sums, out, *, devices, seq):
    half = seq // 2
    parts = three_parts(sums[...] * LOG2E)
    for d in range(devices):
        whole = slice(d * HDIM, (d + 1) * HDIM)
        head = devices + d // 2
        shared = slice(head * HDIM, (head + 1) * HDIM)
        part = slice((d % 2) * half, (d % 2 + 1) * half)
        out[d, 0:seq, :] = queries[:, whole]
        out[d, seq : 2 * seq, :] = keys[:, whole]
        out[d, 2 * seq : 3 * seq, :] = values[:, whole]
        out[d, 3 * seq : 4 * seq, :] = queries[:, shared]
        out[d, 4 * seq : 4 * seq + half, :] = keys[part, shared]
        out[d, 4 * seq + half : 5 * seq, :] = values[part, shared]
        out[d, 5 * seq : 5 * seq + STAT, :] = stat_rows([x[d : d + 1] for x in parts], [x[head : head + 1] for x in parts])


def pack_grads_kernel(meta, near, far, outputs, out, deltas, *, devices, seq):
    half = seq // 2
    tp = meta[2]
    low = pl.ds(pl.multiple_of(tp * half, half), half)
    high = pl.ds(pl.multiple_of((1 - tp) * half, half), half)
    for d in range(devices):
        head = devices + d // 2
        for at, h in ((0, d), (seq, head)):
            cols = slice(h * HDIM, (h + 1) * HDIM)
            if at == 0 or d % 2 == 0:
                out[d, pl.ds(at + pl.multiple_of(tp * half, half), half), :] = near[:, cols]
                out[d, pl.ds(at + pl.multiple_of((1 - tp) * half, half), half), :] = far[:, cols]
                grad_rows = out[d, at : at + seq, :]
                terms = grad_rows.astype(jnp.float32) * outputs[:, cols].astype(jnp.float32)
                deltas[h : h + 1, :] = jnp.sum(terms.T, axis=0, keepdims=True)
            else:
                out[d, at : at + seq, :] = out[d - 1, at : at + seq, :]
    parts = three_parts(deltas[...])
    for d in range(devices):
        head = devices + d // 2
        out[d, 2 * seq : 2 * seq + STAT, :] = stat_rows([x[d : d + 1] for x in parts], [x[head : head + 1] for x in parts])


def attention_kernel(meta, qkv, grads, stat, out, dq_acc, dk_acc, dv_acc, *, blocks, seq, shared):
    half = seq // 2
    part_len = meta[0]
    which = meta[1]
    span = QTILE // seq
    if shared:
        rows, q_at, k_at, v_at, g_at = half, 3 * seq, 4 * seq, 4 * seq + half, seq
    else:
        rows, q_at, k_at, v_at, g_at = seq, 0, seq, 2 * seq, 0
    dq_at, dk_at, dv_at = 0, seq, seq + rows
    key_span = KTILE // rows
    dq_acc[...] = jnp.zeros_like(dq_acc)

    def key_tile(kt, carry):
        first = kt * key_span
        key_rows = qkv[pl.ds(first, key_span), k_at : k_at + rows, :].reshape(KTILE, HDIM)
        value_rows = qkv[pl.ds(first, key_span), v_at : v_at + rows, :].reshape(KTILE, HDIM)
        key_cols = key_rows.T
        index = lax.broadcasted_iota(jnp.int32, (KTILE, 1), 0)
        if shared:
            key_pos = (first + index // rows) * seq + which * rows + index % rows
        else:
            key_pos = first * seq + index
        key_pos = jnp.where(key_pos < part_len, -1, key_pos)
        dk_acc[...] = jnp.zeros_like(dk_acc)
        dv_acc[...] = jnp.zeros_like(dv_acc)

        def query_tile(qt, carry):
            at = qt * span
            query_rows = qkv[pl.ds(at, span), q_at : q_at + seq, :].reshape(QTILE, HDIM)
            grad_rows = grads[pl.ds(at, span), g_at : g_at + seq, :].reshape(QTILE, HDIM)
            log_sum = stat[0, pl.ds(qt, 1), :]
            delta = stat[1, pl.ds(qt, 1), :]
            scores = dot_nt(key_rows, query_rows) * (FACTOR * LOG2E) - log_sum
            query_pos = at * seq + lax.broadcasted_iota(jnp.int32, (1, QTILE), 1)
            weights = jnp.where(key_pos <= query_pos, jnp.exp2(scores), 0.0)
            weight_grads = dot_nt(value_rows, grad_rows)
            score_grads = (weights * (weight_grads - delta) * FACTOR).astype(jnp.bfloat16)
            dv_acc[...] += dot_nn(weights.astype(jnp.bfloat16), grad_rows)
            dk_acc[...] += dot_nn(score_grads, query_rows)
            where = pl.ds(pl.multiple_of(at * seq, QTILE), QTILE)
            dq_acc[:, where] += dot_nn(key_cols, score_grads)
            return carry

        lax.fori_loop(0, blocks // span, query_tile, 0)
        shape = (key_span, rows, HDIM)
        out[pl.ds(first, key_span), dk_at : dk_at + rows, :] = dk_acc[...].astype(jnp.bfloat16).reshape(shape)
        out[pl.ds(first, key_span), dv_at : dv_at + rows, :] = dv_acc[...].astype(jnp.bfloat16).reshape(shape)
        return carry

    lax.fori_loop(0, blocks // key_span, key_tile, 0)
    for b in range(blocks):
        out[b, dq_at : dq_at + seq, :] = dq_acc[:, b * seq : (b + 1) * seq].T.astype(jnp.bfloat16)


def attention(meta, qkv, grads, stat, seq, shared):
    blocks = qkv.shape[0]
    total = blocks * seq
    keys = total // 2 if shared else total
    out_rows = 2 * seq if shared else 3 * seq
    return pl.pallas_call(
        functools.partial(attention_kernel, blocks=blocks, seq=seq, shared=shared),
        out_shape=jax.ShapeDtypeStruct((blocks, out_rows, HDIM), jnp.bfloat16),
        in_specs=[SMEM, VMEM, VMEM, VMEM],
        out_specs=VMEM,
        scratch_shapes=[
            pltpu.VMEM((HDIM, total), jnp.float32),
            pltpu.VMEM((KTILE, HDIM), jnp.float32),
            pltpu.VMEM((KTILE, HDIM), jnp.float32),
        ],
        compiler_params=PARAMS,
        cost_estimate=pl.CostEstimate(
            flops=10 * total * keys * HDIM, bytes_accessed=4 << 20, transcendentals=total * keys
        ),
        name="shared_head" if shared else "whole_head",
    )(meta, qkv, grads, stat.reshape(2, total // QTILE, QTILE))


def unpack_kernel(whole, shared, dq, dk, dv, *, devices, seq):
    half = seq // 2
    for d in range(devices):
        cols = slice(d * HDIM, (d + 1) * HDIM)
        dq[:, cols] = whole[d, 0:seq, :]
        dk[:, cols] = whole[d, seq : 2 * seq, :]
        dv[:, cols] = whole[d, 2 * seq : 3 * seq, :]
        head = devices + d // 2
        cols = slice(head * HDIM, (head + 1) * HDIM)
        if d % 2 == 0:
            both = shared[d, 0:seq, :].astype(jnp.float32) + shared[d + 1, 0:seq, :].astype(jnp.float32)
            dq[:, cols] = both.astype(jnp.bfloat16)
        part = slice((d % 2) * half, (d % 2 + 1) * half)
        dk[part, cols] = shared[d, seq : seq + half, :]
        dv[part, cols] = shared[d, seq + half : 2 * seq, :]


def joined_stat(rows):
    devices, _, seq = rows.shape
    x = rows[:, :6].astype(jnp.float32).reshape(devices, 2, 3, seq)
    x = x[:, :, 0] + x[:, :, 1] + x[:, :, 2]
    return jnp.transpose(x, (1, 0, 2)).reshape(2, devices * seq)


def per_device(next_grad, queries, keys, values, outputs, log_sums, part_length):
    devices = lax.axis_size("ctx")
    sections = lax.axis_size("pp")
    ctx = lax.axis_index("ctx")
    tp = lax.axis_index("tp")
    seq, width = queries.shape[1:]
    meta = jnp.stack([part_length[0], ctx % 2, tp])
    sizes = dict(devices=devices, seq=seq)

    packed = pl.pallas_call(
        functools.partial(pack_kernel, **sizes),
        out_shape=jax.ShapeDtypeStruct((devices, 5 * seq + STAT, HDIM), jnp.bfloat16),
        in_specs=[VMEM] * 4,
        out_specs=VMEM,
        compiler_params=PARAMS,
        name="pack",
    )(queries[0], keys[0], values[0], jnp.transpose(log_sums[0]))
    qkv = lax.all_to_all(packed, "ctx", 0, 0, tiled=True)

    own_cols = lax.dynamic_slice_in_dim(next_grad[0], tp * width, width, 1)
    other_cols = lax.dynamic_slice_in_dim(next_grad[0], (1 - tp) * width, width, 1)
    route = [((p + 1) % sections, p) for p in range(sections)]
    cross = [(2 * a + t, 2 * b + 1 - t) for a, b in route for t in range(2)]
    near = lax.ppermute(own_cols, "pp", route)
    far = lax.ppermute(other_cols, ("pp", "tp"), cross)
    packed_grads = pl.pallas_call(
        functools.partial(pack_grads_kernel, **sizes),
        out_shape=jax.ShapeDtypeStruct((devices, 2 * seq + STAT, HDIM), jnp.bfloat16),
        in_specs=[SMEM] + [VMEM] * 3,
        out_specs=VMEM,
        scratch_shapes=[pltpu.VMEM((width // HDIM, seq), jnp.float32)],
        compiler_params=PARAMS,
        name="pack_grads",
    )(meta, near, far, outputs[0])
    packed_grads, qkv = lax.optimization_barrier((packed_grads, qkv))
    grads = lax.all_to_all(packed_grads, "ctx", 0, 0, tiled=True)

    sums = joined_stat(qkv[:, 5 * seq :])
    deltas = joined_stat(grads[:, 2 * seq :])
    stat = jnp.stack([sums, deltas], axis=1)
    mixed = attention(meta, qkv, grads, stat[1], seq, True)
    back_shared = lax.all_to_all(mixed, "ctx", 0, 0, tiled=True)
    mixed = attention(meta, qkv, grads, stat[0], seq, False)
    back_whole = lax.all_to_all(mixed, "ctx", 0, 0, tiled=True)

    result = jax.ShapeDtypeStruct((seq, width), jnp.bfloat16)
    dq, dk, dv = pl.pallas_call(
        functools.partial(unpack_kernel, **sizes),
        out_shape=(result, result, result),
        in_specs=[VMEM] * 2,
        out_specs=(VMEM,) * 3,
        compiler_params=PARAMS,
        name="unpack",
    )(back_whole, back_shared)
    return dq[None], dk[None], dv[None]


def solution(mesh):
    rows = P("pp", "ctx", "tp")
    return jax.shard_map(
        per_device,
        mesh=mesh,
        in_specs=(P("pp", ("ctx", "tp"), None), rows, rows, rows, rows, rows, P("pp")),
        out_specs=(rows, rows, rows),
        check_vma=False,
    )
```
